256 devices in a mesh: dp: 4 (over y), blk: 32 (over z_lo, x, core), uly: 2 (over z_hi).
Axes of the slice: x: 4, y: 4, z: 8 (z_hi: 2, z_lo: 4; z = z_hi * 4 + z_lo), core: 2. Of those that a mesh axis runs over, the one named last changes fastest.
Arguments:
- queries: bfloat16 [16384, 2560], P(('dp', 'blk', 'uly')), parts along dimension 0, may hold values from -8 to 8, as said below
- keys: bfloat16 [16384, 2560], P(('dp', 'blk', 'uly')), parts along dimension 0, may hold values from -8 to 8, as said below
- values: bfloat16 [16384, 2560], P(('dp', 'blk', 'uly')), parts along dimension 0, may hold values from -6 to 6
- query_tangent: bfloat16 [16384, 2560], P(('dp', 'blk', 'uly')), parts along dimension 0, may hold values from -6 to 6
- key_tangent: bfloat16 [16384, 2560], P(('dp', 'blk', 'uly')), parts along dimension 0, may hold values from -6 to 6
- value_tangent: bfloat16 [16384, 2560], P(('dp', 'blk', 'uly')), parts along dimension 0, may hold values from -6 to 6
Outputs:
- attended: bfloat16 [16384, 2560], P(('dp', 'blk', 'uly')), parts along dimension 0
- attended_tangent: bfloat16 [16384, 2560], P(('dp', 'blk', 'uly')), parts along dimension 0
The draws below stay inside these ranges and needn't reach their ends.
There are 4 independent parts, one for each index of `dp`. The reference program is written for one: setup_inputs(seed, part) draws one part's arguments, and reference() takes and returns one part's arrays. A program takes and returns all parts, laid end to end along the dimension named above; each array names one. Nothing has to cross between parts.
Inputs may be any that keep to these rules, and one draw needn't show every extreme that they name: `queries`: entries are real numbers of order one. `keys`: entries are real numbers of order one.
All inputs are finite; a program needn't handle non-finite values.
Results may differ from the reference program's by a relative error of at most 0.015.
Values may be sent and summed in bfloat16 or wider, within the bound.
A program may use at most 256 MiB of HBM per device.

```python
import jax
import jax.numpy as jnp
from jax import lax

HEADS = 20
HEAD_DIM = 128
SEQ = 4096


def draw_queries(key, part):
    key = jax.random.fold_in(key, 3)
    base = jax.random.normal(key, (SEQ, HEADS * HEAD_DIM))
    return jnp.clip(base, -8.0, 8.0).astype(jnp.bfloat16)


def draw_keys(key, part):
    key = jax.random.fold_in(key, 4)
    base = jax.random.normal(key, (SEQ, HEADS * HEAD_DIM))
    return jnp.clip(base, -8.0, 8.0).astype(jnp.bfloat16)


def block_levels(rng, extent, pieces, least, top_value):
    factor_of, own = 1.0, jax.random.fold_in(rng, 6)
    for dim, blocks in pieces:
        draws = jnp.exp(jax.random.uniform(jax.random.fold_in(own, dim), (blocks,), jnp.float32, least / len(pieces), top_value / len(pieces)))
        factor_of = factor_of * jnp.repeat(draws, extent[dim] // blocks).reshape([-1 if axis == dim else 1 for axis in range(len(extent))])
    return factor_of


def scatter_about(stream_key, shape, scale, limit, shards=(), kind=jnp.bfloat16):
    factor_of = block_levels(stream_key, shape, shards, -0.22, 0.18) if shards else 1.0
    result = jax.random.normal(stream_key, shape, jnp.float32) * scale * factor_of
    return jnp.minimum(jnp.maximum(result, -limit), limit).astype(kind)


def setup_inputs(seed: int = 0, part: int = 0) -> dict:
    key_list = jax.random.split(jax.random.key(seed), 7)
    part_keys = jax.random.split(jax.random.fold_in(key_list[6], part), 7)
    return {
        "queries": draw_queries(jax.random.fold_in(jax.random.fold_in(key_list[6], part), 71), part),
        "keys": draw_keys(jax.random.fold_in(jax.random.fold_in(key_list[6], part), 71), part),
        "values": scatter_about(part_keys[2], (SEQ, HEADS * HEAD_DIM), 1.0, 6.0, ((0, 64),)),
        "query_tangent": scatter_about(part_keys[3], (SEQ, HEADS * HEAD_DIM), 1.0, 6.0, ((0, 64),)),
        "key_tangent": scatter_about(part_keys[4], (SEQ, HEADS * HEAD_DIM), 1.0, 6.0, ((0, 64),)),
        "value_tangent": scatter_about(part_keys[5], (SEQ, HEADS * HEAD_DIM), 1.0, 6.0, ((0, 64),)),
    }


def head_major(block):
    return jnp.moveaxis(block.reshape(SEQ, HEADS, HEAD_DIM), 1, 0)


def one_head(per_items):
    query_head, key_head, value_head, qdot_head, kdot_head, vdot_head = per_items
    score_scale = HEAD_DIM ** -0.5
    scores = jnp.dot(query_head, key_head.T, preferred_element_type=jnp.float32) * score_scale
    score_dot = (jnp.dot(qdot_head, key_head.T, preferred_element_type=jnp.float32)
                 + jnp.dot(query_head, kdot_head.T, preferred_element_type=jnp.float32)) * score_scale
    best_row = jnp.max(scores, axis=1, keepdims=True)
    probs = jnp.exp(scores - best_row)
    totals = jnp.sum(probs, axis=1, keepdims=True)
    weighted = probs * score_dot
    tilt = jnp.sum(weighted, axis=1, keepdims=True)
    probs_low = probs.astype(jnp.bfloat16)
    weighted_low = weighted.astype(jnp.bfloat16)
    primal_sum = jnp.dot(probs_low, value_head, preferred_element_type=jnp.float32)
    tangent_sum = (jnp.dot(weighted_low, value_head, preferred_element_type=jnp.float32)
                   + jnp.dot(probs_low, vdot_head, preferred_element_type=jnp.float32))
    output = primal_sum / totals
    tangent = tangent_sum / totals - output * (tilt / totals)
    return output.astype(jnp.bfloat16), tangent.astype(jnp.bfloat16)


def reference(queries, keys, values, query_tangent, key_tangent, value_tangent):
    stacked = tuple(head_major(member) for member in (queries, keys, values, query_tangent, key_tangent, value_tangent))
    outputs, tangents = lax.map(one_head, stacked)
    attended = jnp.moveaxis(outputs, 0, 1).reshape(SEQ, HEADS * HEAD_DIM)
    attended_tangent = jnp.moveaxis(tangents, 0, 1).reshape(SEQ, HEADS * HEAD_DIM)
    return attended, attended_tangent
```

```python
import functools
import math

import jax
import jax.numpy as jnp
from jax import lax
from jax.experimental import pallas as pl
from jax.experimental.pallas import tpu as pltpu
from jax.sharding import PartitionSpec as P

HEADS = 20
HD = 128
TOK = 64
NZ, NX, NC = 8, 4, 2
KEYS = TOK * NX * NC
QROWS = TOK * NZ
SLOTS = 3
SCALE = HD ** -0.5
TO_LOG2 = SCALE * math.log2(math.e)
LAG_X, LAG_RELAY, LAG_COMPUTE = 2, 4, 6


def head_of(z, slot):
    base = 5 * (z // 2)
    if slot == 0:
        return base + 2
    return base + 3 * lax.rem(z, 2) + (slot - 1)


def head_dyn(z, slot):
    base = 5 * (z // 2)
    return base + jnp.where(slot == 0, 2, 3 * lax.rem(z, 2) + slot - 1)


def dot_t(a, b):
    return lax.dot_general(a, b, (((1,), (1,)), ((), ())), preferred_element_type=jnp.float32)


def dot(a, b):
    return lax.dot_general(a, b, (((1,), (0,)), ((), ())), preferred_element_type=jnp.float32)


def attend(q, kv, m_ref, l_ref, ap_ref, aw_ref):
    s = dot_t(q[:, HD:], kv[:, :HD])
    sd = dot_t(q[:, :], kv[:, : 2 * HD])
    n = s.shape[1]
    best = s[:, :HD]
    for j in range(HD, n, HD):
        best = jnp.maximum(best, s[:, j : j + HD])
    best = jnp.max(best, axis=1, keepdims=True) * TO_LOG2
    m_old = m_ref[...]
    m_new = jnp.maximum(m_old, jnp.broadcast_to(best, m_old.shape))
    alpha = jnp.exp2(m_old - m_new)
    m_ref[...] = m_new
    p = jnp.exp2(s * TO_LOG2 - jnp.concatenate([m_new] * (n // HD), axis=1))
    w = p * sd
    total = p[:, :HD]
    for j in range(HD, n, HD):
        total = total + p[:, j : j + HD]
    v = kv[:, 3 * HD :]
    po = dot(p.astype(jnp.bfloat16), kv[:, 2 * HD :])
    wo = dot(w.astype(jnp.bfloat16), jnp.concatenate([v, jnp.ones_like(v)], axis=1))
    alpha2 = jnp.concatenate([alpha, alpha], axis=1)
    l_ref[...] = l_ref[...] * alpha + total
    ap_ref[...] = ap_ref[...] * alpha2 + po
    aw_ref[...] = aw_ref[...] * alpha2 + wo


def kernel(
    q_hbm, k_hbm, v_hbm, qd_hbm, kd_hbm, vd_hbm, o_ref, t_ref,
    stage, pack_kv, pack_q, kv, qb, ob, m_ref, l_ref, ap_ref, aw_ref,
    load_sem, zkv_s, zkv_r, zq_s, zq_r, x_s, x_r, rel_s, rel_r, sib_s, sib_r, out_s, out_r,
):
    blk, uly = lax.axis_index("blk"), lax.axis_index("uly")
    core = lax.rem(blk, NC)
    x = lax.rem(blk // NC, NX)
    z = uly * 4 + blk // (NC * NX)
    even = lax.rem(z, 2) == 0

    def device(zz, xx, cc):
        return {"blk": (lax.rem(zz, 4) * NX + xx) * NC + cc, "uly": zz // 4}

    def z_peer(dz):
        return lax.rem(z + dz, NZ)

    def x_peer(dx):
        return lax.rem(x + dx, NX)

    other = 1 - core
    sibling = device(z, x, other)
    right, left = device(z, x_peer(1), core), device(z, x_peer(3), core)

    def remote(src, dst, send, recv, to):
        return pltpu.make_async_remote_copy(
            src_ref=src, dst_ref=dst, send_sem=send, recv_sem=recv,
            device_id=to, device_id_type=pl.DeviceIdType.MESH,
        )

    barrier = pltpu.get_barrier_semaphore()
    for dz in range(1, NZ):
        pl.semaphore_signal(barrier, inc=1, device_id=device(z_peer(dz), x, core), device_id_type=pl.DeviceIdType.MESH)
    for to in (sibling, right, left):
        pl.semaphore_signal(barrier, inc=1, device_id=to, device_id_type=pl.DeviceIdType.MESH)

    loads = []
    for i, ref in enumerate((k_hbm, kd_hbm, vd_hbm, v_hbm, qd_hbm, q_hbm)):
        copy = pltpu.make_async_copy(ref, stage.at[i], load_sem.at[i])
        copy.start()
        loads.append(copy)
    for copy in loads:
        copy.wait()

    def pack(h):
        columns = pl.ds(h * HD, HD)
        for i in range(4):
            pack_kv[h, :, i * HD : (i + 1) * HD] = stage[i, :, columns]
        for i in range(2):
            pack_q[h, :, i * HD : (i + 1) * HD] = stage[4 + i, :, columns]

    for h in range(HEADS):
        pack(h)

    def place(xx, cc):
        return pl.ds(pl.multiple_of((xx * NC + cc) * TOK, TOK), TOK)

    mine = place(x, core)
    my_rows = pl.ds(pl.multiple_of(z * TOK, TOK), TOK)

    def own(slot):
        h = head_of(z, slot)
        kv[slot, z, mine, :] = pack_kv[h]
        qb[slot, my_rows, :] = pack_q[h]

    pl.when(even)(lambda: own(0))
    own(1)
    own(2)

    pl.semaphore_wait(barrier, NZ - 1 + 3)

    def send_kv(slot, dz):
        zz = z_peer(dz)
        remote(pack_kv.at[head_of(zz, slot)], kv.at[slot, z, mine], zkv_s.at[slot], zkv_r.at[slot, dz],
               device(zz, x, core)).start()

    def send_q(slot, dz):
        zz = z_peer(dz)
        remote(pack_q.at[head_of(zz, slot)], qb.at[slot, my_rows], zq_s.at[slot], zq_r.at[slot],
               device(zz, x, core)).start()

    def send_all(slot, send):
        for dz in (1, 7, 2, 6, 3, 5, 4):
            if slot == 0:
                pl.when(lax.rem(z + dz, 2) == 0)(functools.partial(send, slot, dz))
            else:
                send(slot, dz)

    send_all(0, send_kv)
    send_all(0, send_q)
    send_all(1, send_kv)
    send_all(1, send_q)
    send_all(2, send_q)
    send_all(2, send_kv)

    toward = jnp.where(core == 0, 1, 3)
    relay_to = device(z, x_peer(toward), core)
    relay_block = place(x_peer(NX - toward), core)
    left_block, right_block, far_block = place(x_peer(3), core), place(x_peer(1), core), place(x_peer(2), core)

    def unpack_step(n):
        slot, i = n // NZ, lax.rem(n, NZ)
        half = (i + 1) // 2
        dz = jnp.where(lax.rem(i, 2) == 1, half, lax.rem(NZ - half, NZ))
        zz = lax.rem(z - dz + NZ, NZ)
        return slot, i, dz, zz

    def to_sibling(slot, i, zz, block):
        ref = kv.at[slot, zz, block]
        remote(ref, ref, sib_s.at[slot], sib_r.at[slot, i], sibling).start()

    def from_z(n):
        slot, i, dz, zz = unpack_step(n)
        ref = kv.at[slot, zz, mine]

        @pl.when(i > 0)
        def _():
            remote(ref, ref, zkv_s.at[slot], zkv_r.at[slot, dz], right).wait_recv()

        remote(ref, ref, x_s.at[slot], x_r.at[slot, i, 0], right).start()
        remote(ref, ref, x_s.at[slot], x_r.at[slot, i, 1], left).start()
        to_sibling(slot, i, zz, mine)

    def from_x(n):
        slot, i, dz, zz = unpack_step(n)
        l_at, r_at, rel = kv.at[slot, zz, left_block], kv.at[slot, zz, right_block], kv.at[slot, zz, relay_block]
        remote(l_at, l_at, x_s.at[slot], x_r.at[slot, i, 0], right).wait_recv()
        remote(r_at, r_at, x_s.at[slot], x_r.at[slot, i, 1], left).wait_recv()
        remote(rel, rel, rel_s.at[slot], rel_r.at[slot, i], relay_to).start()
        to_sibling(slot, i, zz, left_block)
        to_sibling(slot, i, zz, right_block)

    def from_relay(n):
        slot, i, dz, zz = unpack_step(n)
        far = kv.at[slot, zz, far_block]
        remote(far, far, rel_s.at[slot], rel_r.at[slot, i], relay_to).wait_recv()
        to_sibling(slot, i, zz, far_block)

    def compute(n):
        slot, i, dz, zz = unpack_step(n)
        four = kv.at[slot, zz, pl.ds(0, 4 * TOK)]
        remote(four, four, sib_s.at[slot], sib_r.at[slot, i], sibling).wait_recv()

        @pl.when(i == 0)
        def _():
            seven = qb.at[slot, pl.ds(0, QROWS - TOK)]
            remote(seven, seven, zq_s.at[slot], zq_r.at[slot], right).wait_recv()
            m_ref[...] = jnp.full_like(m_ref, -1e30)
            l_ref[...] = jnp.zeros_like(l_ref)
            ap_ref[...] = jnp.zeros_like(ap_ref)
            aw_ref[...] = jnp.zeros_like(aw_ref)

        attend(qb.at[slot], kv.at[slot, zz], m_ref, l_ref, ap_ref, aw_ref)

        @pl.when(i == NZ - 1)
        def _():
            inv = 1.0 / jnp.sum(l_ref[...], axis=1, keepdims=True)
            o = ap_ref[:, HD:] * inv
            tilt = aw_ref[:, HD:] * (SCALE * inv)
            tangent = (ap_ref[:, :HD] + aw_ref[:, :HD] * SCALE) * inv - o * tilt
            ob[slot, 0] = o.astype(jnp.bfloat16)
            ob[slot, 1] = tangent.astype(jnp.bfloat16)
            columns = pl.ds(pl.multiple_of(head_dyn(z, slot) * HD, HD), HD)
            o_ref[:, columns] = ob[slot, 0, my_rows, :]
            t_ref[:, columns] = ob[slot, 1, my_rows, :]
            for dz in (4, 3, 5, 2, 6, 1, 7):
                to_z = z_peer(dz)
                rows = pl.ds(pl.multiple_of(to_z * TOK, TOK), TOK)
                to = device(to_z, x, core)
                remote(ob.at[slot, 0, rows], o_ref.at[:, columns], out_s.at[slot], out_r.at[0], to).start()
                remote(ob.at[slot, 1, rows], t_ref.at[:, columns], out_s.at[slot], out_r.at[1], to).start()

    first = jnp.where(even, 0, NZ)
    last = SLOTS * NZ

    def step(n, carry):
        for lag, do in ((0, from_z), (LAG_X, from_x), (LAG_RELAY, from_relay), (LAG_COMPUTE, compute)):
            pl.when(jnp.logical_and(n - lag >= first, n - lag < last))(functools.partial(do, n - lag))
        return carry

    lax.fori_loop(first, last + LAG_COMPUTE, step, 0)

    def drain_sends(slot):
        z_kv = pack_kv.at[pl.ds(0, NZ - 1)]
        z_q = pack_q.at[pl.ds(0, NZ - 1)]
        if slot > 0:
            remote(z_kv, z_kv, zkv_s.at[slot], zkv_r.at[slot, 1], right).wait_send()
            remote(z_q, z_q, zq_s.at[slot], zq_r.at[slot], right).wait_send()
        x_all, rel_all, sib_all = kv.at[slot, pl.ds(0, 2)], kv.at[slot, 0], kv.at[slot, pl.ds(0, 4)]
        remote(x_all, x_all, x_s.at[slot], x_r.at[slot, 0, 0], right).wait_send()
        remote(rel_all, rel_all, rel_s.at[slot], rel_r.at[slot, 0], right).wait_send()
        remote(sib_all, sib_all, sib_s.at[slot], sib_r.at[slot, 0], right).wait_send()
        out_all = ob.at[slot, :, pl.ds(0, QROWS - TOK)]
        remote(out_all, out_all, out_s.at[slot], out_r.at[0], right).wait_send()

    pl.when(even)(lambda: drain_sends(0))
    drain_sends(1)
    drain_sends(2)

    def drain_parity(targets, foreign):
        z_kv = pack_kv.at[pl.ds(0, targets)]
        z_q = pack_q.at[pl.ds(0, targets)]
        remote(z_kv, z_kv, zkv_s.at[0], zkv_r.at[0, 1], right).wait_send()
        remote(z_q, z_q, zq_s.at[0], zq_r.at[0], right).wait_send()
        o_all, t_all = o_ref.at[:, pl.ds(0, foreign * HD)], t_ref.at[:, pl.ds(0, foreign * HD)]
        remote(o_all, o_all, out_s.at[0], out_r.at[0], right).wait_recv()
        remote(t_all, t_all, out_s.at[0], out_r.at[1], right).wait_recv()

    pl.when(even)(lambda: drain_parity(3, HEADS - 3))
    pl.when(jnp.logical_not(even))(lambda: drain_parity(4, HEADS - 2))


def shards(queries, keys, values, query_tangent, key_tangent, value_tangent):
    out = jax.ShapeDtypeStruct(queries.shape, jnp.bfloat16)
    bf16, f32 = jnp.bfloat16, jnp.float32
    dma = pltpu.SemaphoreType.DMA
    return pl.pallas_call(
        kernel,
        out_shape=(out, out),
        in_specs=[pl.BlockSpec(memory_space=pl.ANY)] * 6,
        out_specs=(pl.BlockSpec(memory_space=pltpu.VMEM),) * 2,
        scratch_shapes=[
            pltpu.VMEM((6, TOK, HEADS * HD), bf16),
            pltpu.VMEM((HEADS, TOK, 4 * HD), bf16),
            pltpu.VMEM((HEADS, TOK, 2 * HD), bf16),
            pltpu.VMEM((SLOTS, NZ, KEYS, 4 * HD), bf16),
            pltpu.VMEM((SLOTS, QROWS, 2 * HD), bf16),
            pltpu.VMEM((SLOTS, 2, QROWS, HD), bf16),
            pltpu.VMEM((QROWS, HD), f32),
            pltpu.VMEM((QROWS, HD), f32),
            pltpu.VMEM((QROWS, 2 * HD), f32),
            pltpu.VMEM((QROWS, 2 * HD), f32),
            dma((6,)),
            dma((SLOTS,)), dma((SLOTS, NZ)),
            dma((SLOTS,)), dma((SLOTS,)),
            dma((SLOTS,)), dma((SLOTS, NZ, 2)),
            dma((SLOTS,)), dma((SLOTS, NZ)),
            dma((SLOTS,)), dma((SLOTS, NZ)),
            dma((SLOTS,)), dma((2,)),
        ],
        compiler_params=pltpu.CompilerParams(
            collective_id=0, has_side_effects=True, vmem_limit_bytes=48 * 2**20
        ),
        cost_estimate=pl.CostEstimate(flops=8 * 10**9, bytes_accessed=3 * 10**6, transcendentals=5 * 10**6),
    )(queries, keys, values, query_tangent, key_tangent, value_tangent)


def solution(mesh):
    spec = P(("dp", "blk", "uly"), None)
    return jax.shard_map(shards, mesh=mesh, in_specs=(spec,) * 6, out_specs=(spec,) * 2, check_vma=False)
```

```python
import functools
import math

import jax
import jax.numpy as jnp
from jax import lax
from jax.experimental import pallas as pl
from jax.experimental.pallas import tpu as pltpu
from jax.sharding import PartitionSpec as P

HEADS = 20
HD = 128
TOK = 64
NZ, NX, NC = 8, 4, 2
KEYS = TOK * NX * NC
QROWS = TOK * NZ
SCALE = HD ** -0.5
TO_LOG2 = SCALE * math.log2(math.e)
LAG_X, LAG_RELAY, LAG_RING, LAG_PAIR = 2, 4, 5, 4
LATE = 12
PAIR, RING = 0, 1
NEAR_FIRST = (1, 7, 2, 6, 3, 5, 4)


def dot_t(a, b):
    return lax.dot_general(a, b, (((1,), (1,)), ((), ())), preferred_element_type=jnp.float32)


def dot(a, b):
    return lax.dot_general(a, b, (((1,), (0,)), ((), ())), preferred_element_type=jnp.float32)


def attend(q, kv, m_ref, l_ref, ap_ref, aw_ref):
    s = dot_t(q[:, HD:], kv[:, :HD])
    sd = dot_t(q[:, :], kv[:, : 2 * HD])
    n = s.shape[1]
    best = s[:, :HD]
    for j in range(HD, n, HD):
        best = jnp.maximum(best, s[:, j : j + HD])
    best = jnp.max(best, axis=1, keepdims=True) * TO_LOG2
    m_old = m_ref[...]
    m_new = jnp.maximum(m_old, jnp.broadcast_to(best, m_old.shape))
    alpha = jnp.exp2(m_old - m_new)
    m_ref[...] = m_new
    p = jnp.exp2(s * TO_LOG2 - jnp.concatenate([m_new] * (n // HD), axis=1))
    w = p * sd
    total = p[:, :HD]
    for j in range(HD, n, HD):
        total = total + p[:, j : j + HD]
    v = kv[:, 3 * HD :]
    po = dot(p.astype(jnp.bfloat16), kv[:, 2 * HD :])
    wo = dot(w.astype(jnp.bfloat16), jnp.concatenate([v, jnp.ones_like(v)], axis=1))
    alpha2 = jnp.concatenate([alpha, alpha], axis=1)
    l_ref[...] = l_ref[...] * alpha + total
    ap_ref[...] = ap_ref[...] * alpha2 + po
    aw_ref[...] = aw_ref[...] * alpha2 + wo


def kernel(
    q_hbm, k_hbm, v_hbm, qd_hbm, kd_hbm, vd_hbm, o_ref, t_ref,
    stage, pack_kv, pack_q, kv, qb, ob, m_ref, l_ref, ap_ref, aw_ref,
    load_sem, zkv_s, zkv_r, zq_s, zq_r, in_s, in_r, x_s, x_r, rel_s, rel_r, sib_s, sib_r, out_s, out_r,
):
    blk, uly = lax.axis_index("blk"), lax.axis_index("uly")
    core = lax.rem(blk, NC)
    x = lax.rem(blk // NC, NX)
    z = uly * 4 + blk // (NC * NX)
    even = lax.rem(z, 2) == 0
    outer_x = NX - 1 - x
    inner_x = x + 1 - 2 * lax.rem(x, 2)
    pair, outer_pair = x // 2, outer_x // 2

    def device(zz, xx, cc):
        return {"blk": (lax.rem(zz, 4) * NX + xx) * NC + cc, "uly": zz // 4}

    def z_peer(dz):
        return lax.rem(z + dz, NZ)

    def pair_head(zz, pp):
        return 5 * (zz // 2) + 3 * lax.rem(zz, 2) + pp

    def ring_head(zz):
        return 5 * (zz // 2) + 2

    sibling = device(z, x, 1 - core)
    inner = device(z, inner_x, core)
    right, left = device(z, lax.rem(x + 1, NX), core), device(z, lax.rem(x + 3, NX), core)

    def remote(src, dst, send, recv, to):
        return pltpu.make_async_remote_copy(
            src_ref=src, dst_ref=dst, send_sem=send, recv_sem=recv,
            device_id=to, device_id_type=pl.DeviceIdType.MESH,
        )

    peers = [device(z_peer(dz), x, core) for dz in range(1, NZ)]
    peers += [device(z_peer(dz), outer_x, core) for dz in range(NZ)]
    peers += [inner, sibling]
    barrier = pltpu.get_barrier_semaphore()
    for to in peers:
        pl.semaphore_signal(barrier, inc=1, device_id=to, device_id_type=pl.DeviceIdType.MESH)

    loads = []
    for i, ref in enumerate((k_hbm, kd_hbm, vd_hbm, v_hbm, qd_hbm, q_hbm)):
        copy = pltpu.make_async_copy(ref, stage.at[i], load_sem.at[i])
        copy.start()
        loads.append(copy)

    ring_heads = range(2, HEADS, 5)
    pair_heads = [h for h in range(HEADS) if h not in ring_heads]

    def pack(into, first, count, heads):
        for h in heads:
            for i in range(count):
                into[h, :, i * HD : (i + 1) * HD] = stage[first + i, :, pl.ds(h * HD, HD)]

    def blocks(first, count):
        return pl.ds(first * TOK, count * TOK)

    my_rows = pl.ds(pl.multiple_of(z * TOK, TOK), TOK)

    def send_ring(dz):
        zz = z_peer(dz)
        remote(pack_kv.at[ring_head(zz)], kv.at[RING, z, blocks(0, 1)], zkv_s.at[RING], zkv_r.at[RING, dz],
               device(zz, x, core)).start()

    def send_ring_q(dz):
        zz = z_peer(dz)
        remote(pack_q.at[ring_head(zz)], qb.at[2, my_rows], zq_s.at[2], zq_r.at[2], device(zz, x, core)).start()

    def to_ring(send):
        for dz in NEAR_FIRST:
            pl.when(lax.rem(z + dz, 2) == 0)(functools.partial(send, dz))

    def keep_ring():
        kv[RING, z, blocks(0, 1), :] = pack_kv[ring_head(z)]

    def keep_ring_q():
        qb[2, my_rows, :] = pack_q[ring_head(z)]

    for copy in loads[:4]:
        copy.wait()
    pack(pack_kv, 0, 4, ring_heads)
    pl.when(even)(keep_ring)
    pl.semaphore_wait(barrier, len(peers))
    to_ring(send_ring)

    for copy in loads[4:]:
        copy.wait()
    pack(pack_q, 4, 2, ring_heads)
    pl.when(even)(keep_ring_q)
    to_ring(send_ring_q)

    pack(pack_q, 4, 2, pair_heads)
    qb[0, my_rows, :] = pack_q[pair_head(z, pair)]
    for dz in NEAR_FIRST:
        zz = z_peer(dz)
        remote(pack_q.at[pair_head(zz, pair)], qb.at[0, my_rows], zq_s.at[0], zq_r.at[0],
               device(zz, x, core)).start()

    pack(pack_kv, 0, 4, pair_heads)
    kv[PAIR, z, blocks(0, 1), :] = pack_kv[pair_head(z, pair)]
    for dz in (0,) + NEAR_FIRST:
        zz = z_peer(dz)
        if dz:
            remote(pack_kv.at[pair_head(zz, pair)], kv.at[PAIR, z, blocks(0, 1)], zkv_s.at[PAIR],
                   zkv_r.at[PAIR, dz], device(zz, x, core)).start()
        remote(pack_kv.at[pair_head(zz, outer_pair)], kv.at[PAIR, z, blocks(1, 1)], zkv_s.at[PAIR],
               zkv_r.at[PAIR, dz], device(zz, outer_x, core)).start()

    def send_outer_q():
        for dz in (0,) + NEAR_FIRST:
            zz = z_peer(dz)
            remote(pack_q.at[pair_head(zz, outer_pair)], qb.at[1, my_rows], zq_s.at[1], zq_r.at[1],
                   device(zz, outer_x, core)).start()

    m_ref[...] = jnp.full_like(m_ref, -1e30)
    l_ref[...] = jnp.zeros_like(l_ref)
    ap_ref[...] = jnp.zeros_like(ap_ref)
    aw_ref[...] = jnp.zeros_like(aw_ref)

    def chunk_of(i):
        half = (i + 1) // 2
        dz = jnp.where(lax.rem(i, 2) == 1, half, lax.rem(NZ - half, NZ))
        return dz, lax.rem(z - dz + NZ, NZ)

    def to_sibling(way, i, zz):
        remote(kv.at[way, zz, blocks(0, 4)], kv.at[way, zz, blocks(4, 4)], sib_s.at[way], sib_r.at[way, i],
               sibling).start()

    def pair_arrived(i):
        dz, zz = chunk_of(i)
        one, two = kv.at[PAIR, zz, blocks(1, 1)], kv.at[PAIR, zz, blocks(0, 2)]

        @pl.when(i == 0)
        def _():
            remote(one, one, zkv_s.at[PAIR], zkv_r.at[PAIR, dz], inner).wait_recv()

        @pl.when(i > 0)
        def _():
            remote(two, two, zkv_s.at[PAIR], zkv_r.at[PAIR, dz], inner).wait_recv()

        remote(two, kv.at[PAIR, zz, blocks(2, 2)], in_s, in_r.at[i], inner).start()

    def pair_from_inner(i):
        dz, zz = chunk_of(i)
        two = kv.at[PAIR, zz, blocks(2, 2)]
        remote(two, two, in_s, in_r.at[i], inner).wait_recv()
        to_sibling(PAIR, i, zz)

    def ring_arrived(i):
        dz, zz = chunk_of(i)
        own = kv.at[RING, zz, blocks(0, 1)]

        @pl.when(i > 0)
        def _():
            remote(own, own, zkv_s.at[RING], zkv_r.at[RING, dz], right).wait_recv()

        remote(own, kv.at[RING, zz, blocks(1, 1)], x_s, x_r.at[i, 0], right).start()
        remote(own, kv.at[RING, zz, blocks(2, 1)], x_s, x_r.at[i, 1], left).start()

    def ring_from_x(i):
        dz, zz = chunk_of(i)
        from_left, from_right, far = (kv.at[RING, zz, blocks(b, 1)] for b in (1, 2, 3))
        remote(from_left, from_left, x_s, x_r.at[i, 0], right).wait_recv()
        remote(from_right, from_right, x_s, x_r.at[i, 1], left).wait_recv()
        pl.when(core == 0)(lambda: remote(from_left, far, rel_s, rel_r.at[i], right).start())
        pl.when(core == 1)(lambda: remote(from_right, far, rel_s, rel_r.at[i], left).start())

    def ring_from_relay(i):
        dz, zz = chunk_of(i)
        far = kv.at[RING, zz, blocks(3, 1)]
        remote(far, far, rel_s, rel_r.at[i], right).wait_recv()
        to_sibling(RING, i, zz)

    def finish(group, head):
        inv = 1.0 / jnp.sum(l_ref[group], axis=1, keepdims=True)
        o = ap_ref[group, :, HD:] * inv
        tilt = aw_ref[group, :, HD:] * (SCALE * inv)
        tangent = (ap_ref[group, :, :HD] + aw_ref[group, :, :HD] * SCALE) * inv - o * tilt
        ob[group, 0] = o.astype(jnp.bfloat16)
        ob[group, 1] = tangent.astype(jnp.bfloat16)
        columns = pl.ds(pl.multiple_of(head * HD, HD), HD)
        to_x = outer_x if group == 1 else x
        if group != 1:
            o_ref[:, columns] = ob[group, 0, my_rows, :]
            t_ref[:, columns] = ob[group, 1, my_rows, :]
        for dz in reversed(NEAR_FIRST + ((0,) if group == 1 else ())):
            to_z = z_peer(dz)
            rows = pl.ds(pl.multiple_of(to_z * TOK, TOK), TOK)
            to = device(to_z, to_x, core)
            remote(ob.at[group, 0, rows], o_ref.at[:, columns], out_s.at[group], out_r.at[0], to).start()
            remote(ob.at[group, 1, rows], t_ref.at[:, columns], out_s.at[group], out_r.at[1], to).start()

    def from_sibling(way, i):
        other = kv.at[way, 0, blocks(4, 4)]
        remote(other, other, sib_s.at[way], sib_r.at[way, i], sibling).wait_recv()

    def add_chunk(group, way, i):
        dz, zz = chunk_of(i)
        attend(qb.at[group], kv.at[way, zz], m_ref.at[group], l_ref.at[group], ap_ref.at[group], aw_ref.at[group])

    seven = qb.at[0, pl.ds(0, QROWS - TOK)]

    def ring_compute(i):
        from_sibling(RING, i)

        @pl.when(i == 0)
        def _():
            remote(seven, seven, zq_s.at[2], zq_r.at[2], inner).wait_recv()

        add_chunk(2, RING, i)
        pl.when(i == NZ - 1)(lambda: finish(2, ring_head(z)))

    def pair_compute(i):
        from_sibling(PAIR, i)

        @pl.when(i == 0)
        def _():
            remote(seven, seven, zq_s.at[0], zq_r.at[0], inner).wait_recv()

        add_chunk(0, PAIR, i)
        pl.when(i == NZ - 1)(lambda: finish(0, pair_head(z, pair)))

    first = jnp.where(even, 0, NZ)

    def step(n, carry):
        pl.when(n == LATE)(send_outer_q)
        for ring_lag, ring_do, pair_lag, pair_do in (
            (0, ring_arrived, 0, pair_arrived),
            (LAG_X, ring_from_x, LAG_X, pair_from_inner),
            (LAG_RELAY, ring_from_relay, None, None),
            (LAG_RING, ring_compute, LAG_PAIR, pair_compute),
        ):
            k = n - ring_lag
            pl.when(jnp.logical_and(k >= first, k < NZ))(functools.partial(ring_do, k))
            if pair_do is not None:
                k = n - pair_lag
                pl.when(jnp.logical_and(k >= NZ, k < 2 * NZ))(functools.partial(pair_do, k - NZ))
        return carry

    lax.fori_loop(first, 2 * NZ + LAG_PAIR, step, 0)

    remote(qb.at[1], qb.at[1], zq_s.at[1], zq_r.at[1], inner).wait_recv()

    def outer_compute(i, carry):
        add_chunk(1, PAIR, i)
        return carry

    lax.fori_loop(0, NZ, outer_compute, 0)
    finish(1, pair_head(z, pair))

    def sent(ref, sem):
        remote(ref, ref, sem, rel_r.at[0], inner).wait_send()

    def arrived(ref, sem):
        remote(ref, ref, load_sem.at[0], sem, inner).wait_recv()

    sent(pack_q.at[pl.ds(0, NZ - 1)], zq_s.at[0])
    sent(pack_q.at[pl.ds(0, NZ)], zq_s.at[1])
    sent(pack_kv.at[pl.ds(0, 2 * NZ - 1)], zkv_s.at[PAIR])
    sent(kv.at[PAIR, pl.ds(0, 2)], in_s)
    sent(kv.at[PAIR, pl.ds(0, 4)], sib_s.at[PAIR])
    sent(ob.at[0, :, pl.ds(0, QROWS - TOK)], out_s.at[0])
    sent(ob.at[1], out_s.at[1])

    def by_parity(targets, foreign):
        sent(pack_kv.at[pl.ds(0, targets)], zkv_s.at[RING])
        sent(pack_q.at[pl.ds(0, targets)], zq_s.at[2])
        arrived(o_ref.at[:, pl.ds(0, foreign * HD)], out_r.at[0])
        arrived(t_ref.at[:, pl.ds(0, foreign * HD)], out_r.at[1])

    @pl.when(even)
    def _():
        sent(kv.at[RING, pl.ds(0, 2)], x_s)
        sent(kv.at[RING, 0], rel_s)
        sent(kv.at[RING, pl.ds(0, 4)], sib_s.at[RING])
        sent(ob.at[2, :, pl.ds(0, QROWS - TOK)], out_s.at[2])
        by_parity(NZ // 2 - 1, HEADS - 2)

    pl.when(jnp.logical_not(even))(lambda: by_parity(NZ // 2, HEADS - 1))


def shards(queries, keys, values, query_tangent, key_tangent, value_tangent):
    out = jax.ShapeDtypeStruct(queries.shape, jnp.bfloat16)
    bf16, f32 = jnp.bfloat16, jnp.float32
    dma = pltpu.SemaphoreType.DMA
    return pl.pallas_call(
        kernel,
        out_shape=(out, out),
        in_specs=[pl.BlockSpec(memory_space=pl.ANY)] * 6,
        out_specs=(pl.BlockSpec(memory_space=pltpu.VMEM),) * 2,
        scratch_shapes=[
            pltpu.VMEM((6, TOK, HEADS * HD), bf16),
            pltpu.VMEM((HEADS, TOK, 4 * HD), bf16),
            pltpu.VMEM((HEADS, TOK, 2 * HD), bf16),
            pltpu.VMEM((2, NZ, KEYS, 4 * HD), bf16),
            pltpu.VMEM((3, QROWS, 2 * HD), bf16),
            pltpu.VMEM((3, 2, QROWS, HD), bf16),
            pltpu.VMEM((3, QROWS, HD), f32),
            pltpu.VMEM((3, QROWS, HD), f32),
            pltpu.VMEM((3, QROWS, 2 * HD), f32),
            pltpu.VMEM((3, QROWS, 2 * HD), f32),
            dma((6,)),
            dma((2,)), dma((2, NZ)),
            dma((3,)), dma((3,)),
            dma, dma((NZ,)),
            dma, dma((NZ, 2)),
            dma, dma((NZ,)),
            dma((2,)), dma((2, NZ)),
            dma((3,)), dma((2,)),
        ],
        compiler_params=pltpu.CompilerParams(
            collective_id=0, has_side_effects=True, vmem_limit_bytes=56 * 2**20
        ),
        cost_estimate=pl.CostEstimate(flops=8 * 10**9, bytes_accessed=3 * 10**6, transcendentals=5 * 10**6),
    )(queries, keys, values, query_tangent, key_tangent, value_tangent)


def solution(mesh):
    spec = P(("dp", "blk", "uly"), None)
    return jax.shard_map(shards, mesh=mesh, in_specs=(spec,) * 6, out_specs=(spec,) * 2, check_vma=False)
```

```python
import functools
import math

import jax
import jax.numpy as jnp
from jax import lax
from jax.experimental import pallas as pl
from jax.experimental.pallas import tpu as pltpu
from jax.sharding import PartitionSpec as P

HEADS = 20
HD = 128
TOK = 64
NZ, NX, NC = 8, 4, 2
KEYS = TOK * NX * NC
QROWS = TOK * NZ
SCALE = HD ** -0.5
TO_LOG2 = SCALE * math.log2(math.e)
LAG_X, LAG_RELAY, LAG_RING, LAG_PAIR = 2, 4, 5, 5
LATE = 14
PAIR, RING = 0, 1
NEAR_FIRST = (1, 7, 2, 6, 3, 5, 4)


def dot_t(a, b):
    return lax.dot_general(a, b, (((1,), (1,)), ((), ())), preferred_element_type=jnp.float32)


def dot(a, b):
    return lax.dot_general(a, b, (((1,), (0,)), ((), ())), preferred_element_type=jnp.float32)


def attend(q, kv, m_ref, l_ref, ap_ref, aw_ref):
    s = dot_t(q[:, HD:], kv[:, :HD])
    sd = dot_t(q[:, :], kv[:, : 2 * HD])
    n = s.shape[1]
    best = s[:, :HD]
    for j in range(HD, n, HD):
        best = jnp.maximum(best, s[:, j : j + HD])
    best = jnp.max(best, axis=1, keepdims=True) * TO_LOG2
    m_old = m_ref[...]
    m_new = jnp.maximum(m_old, jnp.broadcast_to(best, m_old.shape))
    alpha = jnp.exp2(m_old - m_new)
    m_ref[...] = m_new
    p = jnp.exp2(s * TO_LOG2 - jnp.concatenate([m_new] * (n // HD), axis=1))
    w = p * sd
    total = p[:, :HD]
    for j in range(HD, n, HD):
        total = total + p[:, j : j + HD]
    v = kv[:, 3 * HD :]
    po = dot(p.astype(jnp.bfloat16), kv[:, 2 * HD :])
    wo = dot(w.astype(jnp.bfloat16), jnp.concatenate([v, jnp.ones_like(v)], axis=1))
    alpha2 = jnp.concatenate([alpha, alpha], axis=1)
    l_ref[...] = l_ref[...] * alpha + total
    ap_ref[...] = ap_ref[...] * alpha2 + po
    aw_ref[...] = aw_ref[...] * alpha2 + wo


def kernel(
    q_hbm, k_hbm, v_hbm, qd_hbm, kd_hbm, vd_hbm, o_ref, t_ref,
    stage, pack_kv, pack_q, kv, qb, ob, m_ref, l_ref, ap_ref, aw_ref,
    load_sem, zkv_s, zkv_r, zq_s, zq_r, in_s, in_r, x_s, x_r, rel_s, rel_r, sib_s, sib_r, out_s, out_r,
):
    blk, uly = lax.axis_index("blk"), lax.axis_index("uly")
    core = lax.rem(blk, NC)
    x = lax.rem(blk // NC, NX)
    z = uly * 4 + blk // (NC * NX)
    even = lax.rem(z, 2) == 0
    outer_x = NX - 1 - x
    inner_x = x + 1 - 2 * lax.rem(x, 2)
    pair, outer_pair = x // 2, outer_x // 2

    def device(zz, xx, cc):
        return {"blk": (lax.rem(zz, 4) * NX + xx) * NC + cc, "uly": zz // 4}

    def z_peer(dz):
        return lax.rem(z + dz, NZ)

    def pair_head(zz, pp):
        return 5 * (zz // 2) + 3 * lax.rem(zz, 2) + pp

    def ring_head(zz):
        return 5 * (zz // 2) + 2

    sibling = device(z, x, 1 - core)
    inner = device(z, inner_x, core)
    right, left = device(z, lax.rem(x + 1, NX), core), device(z, lax.rem(x + 3, NX), core)

    def remote(src, dst, send, recv, to):
        return pltpu.make_async_remote_copy(
            src_ref=src, dst_ref=dst, send_sem=send, recv_sem=recv,
            device_id=to, device_id_type=pl.DeviceIdType.MESH,
        )

    peers = [device(z_peer(dz), x, core) for dz in range(1, NZ)]
    peers += [device(z_peer(dz), outer_x, core) for dz in range(NZ)]
    peers += [inner, sibling]
    barrier = pltpu.get_barrier_semaphore()
    for to in peers:
        pl.semaphore_signal(barrier, inc=1, device_id=to, device_id_type=pl.DeviceIdType.MESH)

    loads = []
    for i, ref in enumerate((k_hbm, kd_hbm, vd_hbm, v_hbm, qd_hbm, q_hbm)):
        copy = pltpu.make_async_copy(ref, stage.at[i], load_sem.at[i])
        copy.start()
        loads.append(copy)

    ring_heads = range(2, HEADS, 5)
    pair_heads = [h for h in range(HEADS) if h not in ring_heads]

    def pack(into, first, count, heads):
        for h in heads:
            for i in range(count):
                into[h, :, i * HD : (i + 1) * HD] = stage[first + i, :, pl.ds(h * HD, HD)]

    def blocks(first, count):
        return pl.ds(first * TOK, count * TOK)

    my_rows = pl.ds(pl.multiple_of(z * TOK, TOK), TOK)

    def send_ring(dz):
        zz = z_peer(dz)
        remote(pack_kv.at[ring_head(zz)], kv.at[RING, z, blocks(0, 1)], zkv_s.at[RING], zkv_r.at[RING, dz],
               device(zz, x, core)).start()

    def send_ring_q(dz):
        zz = z_peer(dz)
        remote(pack_q.at[ring_head(zz)], qb.at[2, my_rows], zq_s.at[2], zq_r.at[2], device(zz, x, core)).start()

    def to_ring(send):
        for dz in NEAR_FIRST:
            pl.when(lax.rem(z + dz, 2) == 0)(functools.partial(send, dz))

    def keep_ring():
        kv[RING, z, blocks(0, 1), :] = pack_kv[ring_head(z)]

    def keep_ring_q():
        qb[2, my_rows, :] = pack_q[ring_head(z)]

    for copy in loads[:4]:
        copy.wait()
    pack(pack_kv, 0, 4, ring_heads)
    pl.when(even)(keep_ring)
    pl.semaphore_wait(barrier, len(peers))
    to_ring(send_ring)

    for copy in loads[4:]:
        copy.wait()
    pack(pack_q, 4, 2, ring_heads)
    pl.when(even)(keep_ring_q)
    to_ring(send_ring_q)

    pack(pack_kv, 0, 4, pair_heads)
    kv[PAIR, z, blocks(0, 1), :] = pack_kv[pair_head(z, pair)]
    for dz in (0,) + NEAR_FIRST:
        zz = z_peer(dz)
        if dz:
            remote(pack_kv.at[pair_head(zz, pair)], kv.at[PAIR, z, blocks(0, 1)], zkv_s.at[PAIR],
                   zkv_r.at[PAIR, dz], device(zz, x, core)).start()
        remote(pack_kv.at[pair_head(zz, outer_pair)], kv.at[PAIR, z, blocks(1, 1)], zkv_s.at[PAIR],
               zkv_r.at[PAIR, dz], device(zz, outer_x, core)).start()

    pack(pack_q, 4, 2, pair_heads)
    qb[0, my_rows, :] = pack_q[pair_head(z, pair)]
    for dz in NEAR_FIRST:
        zz = z_peer(dz)
        remote(pack_q.at[pair_head(zz, pair)], qb.at[0, my_rows], zq_s.at[0], zq_r.at[0],
               device(zz, x, core)).start()

    def send_outer_q():
        for dz in (0,) + NEAR_FIRST:
            zz = z_peer(dz)
            remote(pack_q.at[pair_head(zz, outer_pair)], qb.at[1, my_rows], zq_s.at[1], zq_r.at[1],
                   device(zz, outer_x, core)).start()

    m_ref[...] = jnp.full_like(m_ref, -1e30)
    l_ref[...] = jnp.zeros_like(l_ref)
    ap_ref[...] = jnp.zeros_like(ap_ref)
    aw_ref[...] = jnp.zeros_like(aw_ref)

    def chunk_of(i):
        half = (i + 1) // 2
        dz = jnp.where(lax.rem(i, 2) == 1, half, lax.rem(NZ - half, NZ))
        return dz, lax.rem(z - dz + NZ, NZ)

    def to_sibling(way, i, zz):
        remote(kv.at[way, zz, blocks(0, 4)], kv.at[way, zz, blocks(4, 4)], sib_s.at[way], sib_r.at[way, i],
               sibling).start()

    def pair_arrived(i):
        dz, zz = chunk_of(i)
        one, two = kv.at[PAIR, zz, blocks(1, 1)], kv.at[PAIR, zz, blocks(0, 2)]

        @pl.when(i == 0)
        def _():
            remote(one, one, zkv_s.at[PAIR], zkv_r.at[PAIR, dz], inner).wait_recv()

        @pl.when(i > 0)
        def _():
            remote(two, two, zkv_s.at[PAIR], zkv_r.at[PAIR, dz], inner).wait_recv()

        remote(two, kv.at[PAIR, zz, blocks(2, 2)], in_s, in_r.at[i], inner).start()

    def pair_from_inner(i):
        dz, zz = chunk_of(i)
        two = kv.at[PAIR, zz, blocks(2, 2)]
        remote(two, two, in_s, in_r.at[i], inner).wait_recv()
        to_sibling(PAIR, i, zz)

    def ring_arrived(i):
        dz, zz = chunk_of(i)
        own = kv.at[RING, zz, blocks(0, 1)]

        @pl.when(i > 0)
        def _():
            remote(own, own, zkv_s.at[RING], zkv_r.at[RING, dz], right).wait_recv()

        remote(own, kv.at[RING, zz, blocks(1, 1)], x_s, x_r.at[i, 0], right).start()
        remote(own, kv.at[RING, zz, blocks(2, 1)], x_s, x_r.at[i, 1], left).start()

    def ring_from_x(i):
        dz, zz = chunk_of(i)
        from_left, from_right, far = (kv.at[RING, zz, blocks(b, 1)] for b in (1, 2, 3))
        remote(from_left, from_left, x_s, x_r.at[i, 0], right).wait_recv()
        remote(from_right, from_right, x_s, x_r.at[i, 1], left).wait_recv()
        pl.when(core == 0)(lambda: remote(from_left, far, rel_s, rel_r.at[i], right).start())
        pl.when(core == 1)(lambda: remote(from_right, far, rel_s, rel_r.at[i], left).start())

    def ring_from_relay(i):
        dz, zz = chunk_of(i)
        far = kv.at[RING, zz, blocks(3, 1)]
        remote(far, far, rel_s, rel_r.at[i], right).wait_recv()
        to_sibling(RING, i, zz)

    def finish(group, head):
        inv = 1.0 / jnp.sum(l_ref[group], axis=1, keepdims=True)
        o = ap_ref[group, :, HD:] * inv
        tilt = aw_ref[group, :, HD:] * (SCALE * inv)
        tangent = (ap_ref[group, :, :HD] + aw_ref[group, :, :HD] * SCALE) * inv - o * tilt
        ob[group, 0] = o.astype(jnp.bfloat16)
        ob[group, 1] = tangent.astype(jnp.bfloat16)
        columns = pl.ds(pl.multiple_of(head * HD, HD), HD)
        to_x = outer_x if group == 1 else x
        if group != 1:
            o_ref[:, columns] = ob[group, 0, my_rows, :]
            t_ref[:, columns] = ob[group, 1, my_rows, :]
        for dz in reversed(NEAR_FIRST + ((0,) if group == 1 else ())):
            to_z = z_peer(dz)
            rows = pl.ds(pl.multiple_of(to_z * TOK, TOK), TOK)
            to = device(to_z, to_x, core)
            remote(ob.at[group, 0, rows], o_ref.at[:, columns], out_s.at[group], out_r.at[0], to).start()
            remote(ob.at[group, 1, rows], t_ref.at[:, columns], out_s.at[group], out_r.at[1], to).start()

    def from_sibling(way, i):
        other = kv.at[way, 0, blocks(4, 4)]
        remote(other, other, sib_s.at[way], sib_r.at[way, i], sibling).wait_recv()

    def add_chunk(group, way, i):
        dz, zz = chunk_of(i)
        attend(qb.at[group], kv.at[way, zz], m_ref.at[group], l_ref.at[group], ap_ref.at[group], aw_ref.at[group])

    seven = qb.at[0, pl.ds(0, QROWS - TOK)]

    def ring_compute(i):
        from_sibling(RING, i)

        @pl.when(i == 0)
        def _():
            remote(seven, seven, zq_s.at[2], zq_r.at[2], inner).wait_recv()

        add_chunk(2, RING, i)
        pl.when(i == NZ - 1)(lambda: finish(2, ring_head(z)))

    def pair_compute(i):
        from_sibling(PAIR, i)

        @pl.when(i == 0)
        def _():
            remote(seven, seven, zq_s.at[0], zq_r.at[0], inner).wait_recv()

        add_chunk(0, PAIR, i)
        pl.when(i == NZ - 1)(lambda: finish(0, pair_head(z, pair)))

    first = jnp.where(even, 0, NZ)

    def step(n, carry):
        pl.when(n == LATE)(send_outer_q)
        for ring_lag, ring_do, pair_lag, pair_do in (
            (0, ring_arrived, 0, pair_arrived),
            (LAG_X, ring_from_x, LAG_X, pair_from_inner),
            (LAG_RELAY, ring_from_relay, None, None),
            (LAG_RING, ring_compute, LAG_PAIR, pair_compute),
        ):
            k = n - ring_lag
            pl.when(jnp.logical_and(k >= first, k < NZ))(functools.partial(ring_do, k))
            if pair_do is not None:
                k = n - pair_lag
                pl.when(jnp.logical_and(k >= NZ, k < 2 * NZ))(functools.partial(pair_do, k - NZ))
        return carry

    lax.fori_loop(first, 2 * NZ + LAG_PAIR, step, 0)

    remote(qb.at[1], qb.at[1], zq_s.at[1], zq_r.at[1], inner).wait_recv()

    def outer_compute(i, carry):
        add_chunk(1, PAIR, i)
        return carry

    lax.fori_loop(0, NZ, outer_compute, 0)
    finish(1, pair_head(z, pair))

    def sent(ref, sem):
        remote(ref, ref, sem, rel_r.at[0], inner).wait_send()

    def arrived(ref, sem):
        remote(ref, ref, load_sem.at[0], sem, inner).wait_recv()

    sent(pack_q.at[pl.ds(0, NZ - 1)], zq_s.at[0])
    sent(pack_q.at[pl.ds(0, NZ)], zq_s.at[1])
    sent(pack_kv.at[pl.ds(0, 2 * NZ - 1)], zkv_s.at[PAIR])
    sent(kv.at[PAIR, pl.ds(0, 2)], in_s)
    sent(kv.at[PAIR, pl.ds(0, 4)], sib_s.at[PAIR])
    sent(ob.at[0, :, pl.ds(0, QROWS - TOK)], out_s.at[0])
    sent(ob.at[1], out_s.at[1])

    def by_parity(targets, foreign):
        sent(pack_kv.at[pl.ds(0, targets)], zkv_s.at[RING])
        sent(pack_q.at[pl.ds(0, targets)], zq_s.at[2])
        arrived(o_ref.at[:, pl.ds(0, foreign * HD)], out_r.at[0])
        arrived(t_ref.at[:, pl.ds(0, foreign * HD)], out_r.at[1])

    @pl.when(even)
    def _():
        sent(kv.at[RING, pl.ds(0, 2)], x_s)
        sent(kv.at[RING, 0], rel_s)
        sent(kv.at[RING, pl.ds(0, 4)], sib_s.at[RING])
        sent(ob.at[2, :, pl.ds(0, QROWS - TOK)], out_s.at[2])
        by_parity(NZ // 2 - 1, HEADS - 2)

    pl.when(jnp.logical_not(even))(lambda: by_parity(NZ // 2, HEADS - 1))


def shards(queries, keys, values, query_tangent, key_tangent, value_tangent):
    out = jax.ShapeDtypeStruct(queries.shape, jnp.bfloat16)
    bf16, f32 = jnp.bfloat16, jnp.float32
    dma = pltpu.SemaphoreType.DMA
    return pl.pallas_call(
        kernel,
        out_shape=(out, out),
        in_specs=[pl.BlockSpec(memory_space=pl.ANY)] * 6,
        out_specs=(pl.BlockSpec(memory_space=pltpu.VMEM),) * 2,
        scratch_shapes=[
            pltpu.VMEM((6, TOK, HEADS * HD), bf16),
            pltpu.VMEM((HEADS, TOK, 4 * HD), bf16),
            pltpu.VMEM((HEADS, TOK, 2 * HD), bf16),
            pltpu.VMEM((2, NZ, KEYS, 4 * HD), bf16),
            pltpu.VMEM((3, QROWS, 2 * HD), bf16),
            pltpu.VMEM((3, 2, QROWS, HD), bf16),
            pltpu.VMEM((3, QROWS, HD), f32),
            pltpu.VMEM((3, QROWS, HD), f32),
            pltpu.VMEM((3, QROWS, 2 * HD), f32),
            pltpu.VMEM((3, QROWS, 2 * HD), f32),
            dma((6,)),
            dma((2,)), dma((2, NZ)),
            dma((3,)), dma((3,)),
            dma, dma((NZ,)),
            dma, dma((NZ, 2)),
            dma, dma((NZ,)),
            dma((2,)), dma((2, NZ)),
            dma((3,)), dma((2,)),
        ],
        compiler_params=pltpu.CompilerParams(
            collective_id=0, has_side_effects=True, vmem_limit_bytes=213 * 2**18
        ),
        cost_estimate=pl.CostEstimate(flops=8 * 10**9, bytes_accessed=3 * 10**6, transcendentals=5 * 10**6),
    )(queries, keys, values, query_tangent, key_tangent, value_tangent)


def solution(mesh):
    spec = P(("dp", "blk", "uly"), None)
    return jax.shard_map(shards, mesh=mesh, in_specs=(spec,) * 6, out_specs=(spec,) * 2, check_vma=False)
```

```python
import functools
import math

import jax
import jax.numpy as jnp
from jax import lax
from jax.experimental import pallas as pl
from jax.experimental.pallas import tpu as pltpu
from jax.sharding import PartitionSpec as P

HEADS = 20
HD = 128
TOK = 64
NZ, NX, NC = 8, 4, 2
KEYS = TOK * NX * NC
QROWS = TOK * NZ
SCALE = HD ** -0.5
TO_LOG2 = SCALE * math.log2(math.e)
LAG_X, LAG_RELAY, LAG_RING, LAG_PAIR = 2, 4, 5, 5
LATE = 14
PAIR, RING = 0, 1
NEAR_FIRST = (1, 7, 2, 6, 3, 5, 4)


def dot_t(a, b):
    return lax.dot_general(a, b, (((1,), (1,)), ((), ())), preferred_element_type=jnp.float32)


def dot(a, b):
    return lax.dot_general(a, b, (((1,), (0,)), ((), ())), preferred_element_type=jnp.float32)


def attend(q, kv, m_ref, l_ref, ap_ref, aw_ref):
    s = dot_t(q[:, HD:], kv[:, :HD])
    sd = dot_t(q[:, :], kv[:, : 2 * HD])
    n = s.shape[1]
    best = s[:, :HD]
    for j in range(HD, n, HD):
        best = jnp.maximum(best, s[:, j : j + HD])
    best = jnp.max(best, axis=1, keepdims=True) * TO_LOG2
    m_old = m_ref[...]
    m_new = jnp.maximum(m_old, jnp.broadcast_to(best, m_old.shape))
    alpha = jnp.exp2(m_old - m_new)
    m_ref[...] = m_new
    p = jnp.exp2(s * TO_LOG2 - jnp.concatenate([m_new] * (n // HD), axis=1))
    w = p * sd
    total = p[:, :HD]
    for j in range(HD, n, HD):
        total = total + p[:, j : j + HD]
    v = kv[:, 3 * HD :]
    po = dot(p.astype(jnp.bfloat16), kv[:, 2 * HD :])
    wo = dot(w.astype(jnp.bfloat16), jnp.concatenate([v, jnp.ones_like(v)], axis=1))
    alpha2 = jnp.concatenate([alpha, alpha], axis=1)
    l_ref[...] = l_ref[...] * alpha + total
    ap_ref[...] = ap_ref[...] * alpha2 + po
    aw_ref[...] = aw_ref[...] * alpha2 + wo


def kernel(
    q_hbm, k_hbm, v_hbm, qd_hbm, kd_hbm, vd_hbm, o_ref, t_ref,
    stage, pack_kv, pack_q, kv, qb, ob, m_ref, l_ref, ap_ref, aw_ref,
    load_sem, zkv_s, zkv_r, zq_s, zq_r, in_s, in_r, x_s, x_r, rel_s, rel_r, sib_s, sib_r, out_s, out_r,
):
    blk, uly = lax.axis_index("blk"), lax.axis_index("uly")
    core = lax.rem(blk, NC)
    x = lax.rem(blk // NC, NX)
    z = uly * 4 + blk // (NC * NX)
    even = lax.rem(z, 2) == 0
    outer_x = NX - 1 - x
    inner_x = x + 1 - 2 * lax.rem(x, 2)
    pair, outer_pair = x // 2, outer_x // 2

    def device(zz, xx, cc):
        return {"blk": (lax.rem(zz, 4) * NX + xx) * NC + cc, "uly": zz // 4}

    def z_peer(dz):
        return lax.rem(z + dz, NZ)

    def pair_head(zz, pp):
        return 5 * (zz // 2) + 3 * lax.rem(zz, 2) + pp

    def ring_head(zz):
        return 5 * (zz // 2) + 2

    sibling = device(z, x, 1 - core)
    inner = device(z, inner_x, core)
    right, left = device(z, lax.rem(x + 1, NX), core), device(z, lax.rem(x + 3, NX), core)

    def remote(src, dst, send, recv, to):
        return pltpu.make_async_remote_copy(
            src_ref=src, dst_ref=dst, send_sem=send, recv_sem=recv,
            device_id=to, device_id_type=pl.DeviceIdType.MESH,
        )

    peers = [device(z_peer(dz), x, core) for dz in range(1, NZ)]
    peers += [device(z_peer(dz), outer_x, core) for dz in range(NZ)]
    peers += [inner, sibling]
    barrier = pltpu.get_barrier_semaphore()
    for to in peers:
        pl.semaphore_signal(barrier, inc=1, device_id=to, device_id_type=pl.DeviceIdType.MESH)

    loads = []
    for i, ref in enumerate((k_hbm, kd_hbm, vd_hbm, v_hbm, qd_hbm, q_hbm)):
        copy = pltpu.make_async_copy(ref, stage.at[i], load_sem.at[i])
        copy.start()
        loads.append(copy)

    ring_heads = range(2, HEADS, 5)
    pair_heads = [h for h in range(HEADS) if h not in ring_heads]

    def pack(into, first, count, heads):
        for h in heads:
            for i in range(count):
                into[h, :, i * HD : (i + 1) * HD] = stage[first + i, :, pl.ds(h * HD, HD)]

    def blocks(first, count):
        return pl.ds(first * TOK, count * TOK)

    my_rows = pl.ds(pl.multiple_of(z * TOK, TOK), TOK)

    def send_ring(dz):
        zz = z_peer(dz)
        remote(pack_kv.at[ring_head(zz)], kv.at[RING, z, blocks(0, 1)], zkv_s.at[RING], zkv_r.at[RING, dz],
               device(zz, x, core)).start()

    def send_ring_q(dz):
        zz = z_peer(dz)
        remote(pack_q.at[ring_head(zz)], qb.at[2, my_rows], zq_s.at[2], zq_r.at[2], device(zz, x, core)).start()

    def to_ring(send):
        for dz in NEAR_FIRST:
            pl.when(lax.rem(z + dz, 2) == 0)(functools.partial(send, dz))

    def keep_ring():
        kv[RING, z, blocks(0, 1), :] = pack_kv[ring_head(z)]

    def keep_ring_q():
        qb[2, my_rows, :] = pack_q[ring_head(z)]

    for copy in loads[:4]:
        copy.wait()
    pack(pack_kv, 0, 4, ring_heads)
    pl.when(even)(keep_ring)
    pl.semaphore_wait(barrier, len(peers))
    to_ring(send_ring)

    for copy in loads[4:]:
        copy.wait()
    pack(pack_q, 4, 2, ring_heads)
    pl.when(even)(keep_ring_q)
    to_ring(send_ring_q)

    pack(pack_kv, 0, 4, pair_heads)
    kv[PAIR, z, blocks(0, 1), :] = pack_kv[pair_head(z, pair)]
    for dz in (0,) + NEAR_FIRST:
        zz = z_peer(dz)
        if dz:
            remote(pack_kv.at[pair_head(zz, pair)], kv.at[PAIR, z, blocks(0, 1)], zkv_s.at[PAIR],
                   zkv_r.at[PAIR, dz], device(zz, x, core)).start()
        remote(pack_kv.at[pair_head(zz, outer_pair)], kv.at[PAIR, z, blocks(1, 1)], zkv_s.at[PAIR],
               zkv_r.at[PAIR, dz], device(zz, outer_x, core)).start()

    pack(pack_q, 4, 2, pair_heads)
    qb[0, my_rows, :] = pack_q[pair_head(z, pair)]
    for dz in NEAR_FIRST:
        zz = z_peer(dz)
        remote(pack_q.at[pair_head(zz, pair)], qb.at[0, my_rows], zq_s.at[0], zq_r.at[0],
               device(zz, x, core)).start()

    def send_outer_q():
        for dz in (0,) + NEAR_FIRST:
            zz = z_peer(dz)
            remote(pack_q.at[pair_head(zz, outer_pair)], qb.at[1, my_rows], zq_s.at[1], zq_r.at[1],
                   device(zz, outer_x, core)).start()

    m_ref[...] = jnp.full_like(m_ref, -1e30)
    l_ref[...] = jnp.zeros_like(l_ref)
    ap_ref[...] = jnp.zeros_like(ap_ref)
    aw_ref[...] = jnp.zeros_like(aw_ref)

    def chunk_of(i):
        half = (i + 1) // 2
        dz = jnp.where(lax.rem(i, 2) == 1, half, lax.rem(NZ - half, NZ))
        return dz, lax.rem(z - dz + NZ, NZ)

    def to_sibling(way, i, zz):
        remote(kv.at[way, zz, blocks(0, 4)], kv.at[way, zz, blocks(4, 4)], sib_s.at[way], sib_r.at[way, i],
               sibling).start()

    def pair_arrived(i):
        dz, zz = chunk_of(i)
        one, two = kv.at[PAIR, zz, blocks(1, 1)], kv.at[PAIR, zz, blocks(0, 2)]

        @pl.when(i == 0)
        def _():
            remote(one, one, zkv_s.at[PAIR], zkv_r.at[PAIR, dz], inner).wait_recv()

        @pl.when(i > 0)
        def _():
            remote(two, two, zkv_s.at[PAIR], zkv_r.at[PAIR, dz], inner).wait_recv()

        remote(two, kv.at[PAIR, zz, blocks(2, 2)], in_s, in_r.at[i], inner).start()

    def pair_from_inner(i):
        dz, zz = chunk_of(i)
        two = kv.at[PAIR, zz, blocks(2, 2)]
        remote(two, two, in_s, in_r.at[i], inner).wait_recv()
        to_sibling(PAIR, i, zz)

    def ring_arrived(i):
        dz, zz = chunk_of(i)
        own = kv.at[RING, zz, blocks(0, 1)]

        @pl.when(i > 0)
        def _():
            remote(own, own, zkv_s.at[RING], zkv_r.at[RING, dz], right).wait_recv()

        remote(own, kv.at[RING, zz, blocks(1, 1)], x_s, x_r.at[i, 0], right).start()
        remote(own, kv.at[RING, zz, blocks(2, 1)], x_s, x_r.at[i, 1], left).start()

    def ring_from_x(i):
        dz, zz = chunk_of(i)
        from_left, from_right, far = (kv.at[RING, zz, blocks(b, 1)] for b in (1, 2, 3))
        remote(from_left, from_left, x_s, x_r.at[i, 0], right).wait_recv()
        remote(from_right, from_right, x_s, x_r.at[i, 1], left).wait_recv()
        pl.when(core == 0)(lambda: remote(from_left, far, rel_s, rel_r.at[i], right).start())
        pl.when(core == 1)(lambda: remote(from_right, far, rel_s, rel_r.at[i], left).start())

    def ring_from_relay(i):
        dz, zz = chunk_of(i)
        far = kv.at[RING, zz, blocks(3, 1)]
        remote(far, far, rel_s, rel_r.at[i], right).wait_recv()
        to_sibling(RING, i, zz)

    def finish(group, head):
        inv = 1.0 / jnp.sum(l_ref[group], axis=1, keepdims=True)
        o = ap_ref[group, :, HD:] * inv
        tilt = aw_ref[group, :, HD:] * (SCALE * inv)
        tangent = (ap_ref[group, :, :HD] + aw_ref[group, :, :HD] * SCALE) * inv - o * tilt
        ob[group, 0] = o.astype(jnp.bfloat16)
        ob[group, 1] = tangent.astype(jnp.bfloat16)
        columns = pl.ds(pl.multiple_of(head * HD, HD), HD)
        to_x = outer_x if group == 1 else x
        if group != 1:
            o_ref[:, columns] = ob[group, 0, my_rows, :]
            t_ref[:, columns] = ob[group, 1, my_rows, :]
        for dz in reversed(NEAR_FIRST + ((0,) if group == 1 else ())):
            to_z = z_peer(dz)
            rows = pl.ds(pl.multiple_of(to_z * TOK, TOK), TOK)
            to = device(to_z, to_x, core)
            remote(ob.at[group, 0, rows], o_ref.at[:, columns], out_s.at[group], out_r.at[0], to).start()
            remote(ob.at[group, 1, rows], t_ref.at[:, columns], out_s.at[group], out_r.at[1], to).start()

    def from_sibling(way, i):
        other = kv.at[way, 0, blocks(4, 4)]
        remote(other, other, sib_s.at[way], sib_r.at[way, i], sibling).wait_recv()

    def add_chunk(group, way, i):
        dz, zz = chunk_of(i)
        attend(qb.at[group], kv.at[way, zz], m_ref.at[group], l_ref.at[group], ap_ref.at[group], aw_ref.at[group])

    seven = qb.at[0, pl.ds(0, QROWS - TOK)]

    def ring_compute(i):
        from_sibling(RING, i)

        @pl.when(i == 0)
        def _():
            remote(seven, seven, zq_s.at[2], zq_r.at[2], inner).wait_recv()

        add_chunk(2, RING, i)
        pl.when(i == NZ - 1)(lambda: finish(2, ring_head(z)))

    def pair_compute(i):
        from_sibling(PAIR, i)

        @pl.when(i == 0)
        def _():
            remote(seven, seven, zq_s.at[0], zq_r.at[0], inner).wait_recv()

        add_chunk(0, PAIR, i)
        pl.when(i == NZ - 1)(lambda: finish(0, pair_head(z, pair)))

    first = jnp.where(even, 0, NZ)

    def step(n, carry):
        pl.when(n == LATE)(send_outer_q)
        for ring_lag, ring_do, pair_lag, pair_do in (
            (0, ring_arrived, 0, pair_arrived),
            (LAG_X, ring_from_x, LAG_X, pair_from_inner),
            (LAG_RELAY, ring_from_relay, None, None),
            (LAG_RING, ring_compute, LAG_PAIR, pair_compute),
        ):
            k = n - ring_lag
            pl.when(jnp.logical_and(k >= first, k < NZ))(functools.partial(ring_do, k))
            if pair_do is not None:
                k = n - pair_lag
                pl.when(jnp.logical_and(k >= NZ, k < 2 * NZ))(functools.partial(pair_do, k - NZ))
        return carry

    lax.fori_loop(first, 2 * NZ + LAG_PAIR, step, 0)

    remote(qb.at[1], qb.at[1], zq_s.at[1], zq_r.at[1], inner).wait_recv()

    def outer_compute(i, carry):
        add_chunk(1, PAIR, 2 * i)
        add_chunk(1, PAIR, 2 * i + 1)
        return carry

    lax.fori_loop(0, NZ // 2, outer_compute, 0)
    finish(1, pair_head(z, pair))

    def sent(ref, sem):
        remote(ref, ref, sem, rel_r.at[0], inner).wait_send()

    def arrived(ref, sem):
        remote(ref, ref, load_sem.at[0], sem, inner).wait_recv()

    sent(pack_q.at[pl.ds(0, NZ - 1)], zq_s.at[0])
    sent(pack_q.at[pl.ds(0, NZ)], zq_s.at[1])
    sent(pack_kv.at[pl.ds(0, 2 * NZ - 1)], zkv_s.at[PAIR])
    sent(kv.at[PAIR, pl.ds(0, 2)], in_s)
    sent(kv.at[PAIR, pl.ds(0, 4)], sib_s.at[PAIR])
    sent(ob.at[0, :, pl.ds(0, QROWS - TOK)], out_s.at[0])
    sent(ob.at[1], out_s.at[1])

    def by_parity(targets, foreign):
        sent(pack_kv.at[pl.ds(0, targets)], zkv_s.at[RING])
        sent(pack_q.at[pl.ds(0, targets)], zq_s.at[2])
        arrived(o_ref.at[:, pl.ds(0, foreign * HD)], out_r.at[0])
        arrived(t_ref.at[:, pl.ds(0, foreign * HD)], out_r.at[1])

    @pl.when(even)
    def _():
        sent(kv.at[RING, pl.ds(0, 2)], x_s)
        sent(kv.at[RING, 0], rel_s)
        sent(kv.at[RING, pl.ds(0, 4)], sib_s.at[RING])
        sent(ob.at[2, :, pl.ds(0, QROWS - TOK)], out_s.at[2])
        by_parity(NZ // 2 - 1, HEADS - 2)

    pl.when(jnp.logical_not(even))(lambda: by_parity(NZ // 2, HEADS - 1))


def shards(queries, keys, values, query_tangent, key_tangent, value_tangent):
    out = jax.ShapeDtypeStruct(queries.shape, jnp.bfloat16)
    bf16, f32 = jnp.bfloat16, jnp.float32
    dma = pltpu.SemaphoreType.DMA
    return pl.pallas_call(
        kernel,
        out_shape=(out, out),
        in_specs=[pl.BlockSpec(memory_space=pl.ANY)] * 6,
        out_specs=(pl.BlockSpec(memory_space=pltpu.VMEM),) * 2,
        scratch_shapes=[
            pltpu.VMEM((6, TOK, HEADS * HD), bf16),
            pltpu.VMEM((HEADS, TOK, 4 * HD), bf16),
            pltpu.VMEM((HEADS, TOK, 2 * HD), bf16),
            pltpu.VMEM((2, NZ, KEYS, 4 * HD), bf16),
            pltpu.VMEM((3, QROWS, 2 * HD), bf16),
            pltpu.VMEM((3, 2, QROWS, HD), bf16),
            pltpu.VMEM((3, QROWS, HD), f32),
            pltpu.VMEM((3, QROWS, HD), f32),
            pltpu.VMEM((3, QROWS, 2 * HD), f32),
            pltpu.VMEM((3, QROWS, 2 * HD), f32),
            dma((6,)),
            dma((2,)), dma((2, NZ)),
            dma((3,)), dma((3,)),
            dma, dma((NZ,)),
            dma, dma((NZ, 2)),
            dma, dma((NZ,)),
            dma((2,)), dma((2, NZ)),
            dma((3,)), dma((2,)),
        ],
        compiler_params=pltpu.CompilerParams(
            collective_id=0, has_side_effects=True, vmem_limit_bytes=213 * 2**18
        ),
        cost_estimate=pl.CostEstimate(flops=8 * 10**9, bytes_accessed=3 * 10**6, transcendentals=5 * 10**6),
    )(queries, keys, values, query_tangent, key_tangent, value_tangent)


def solution(mesh):
    spec = P(("dp", "blk", "uly"), None)
    return jax.shard_map(shards, mesh=mesh, in_specs=(spec,) * 6, out_specs=(spec,) * 2, check_vma=False)
```
